256 devices in a mesh: segment: 4 (over x), tile: 64 (over z, y, core).
Axes of the slice: x: 4, y: 4, z: 8, core: 2. Of those that a mesh axis runs over, the one named last changes fastest.
Arguments:
- latent_clips: bfloat16 [4, 2, 256, 128, 128], P('segment', None, 'tile'), may hold values from -1.5 to 1.5
- augment_noise: bfloat16 [4, 4, 2, 256, 128, 128], P('segment', None, None, 'tile'), may hold values from -3.59375 to 3.59375
- section_weights: bfloat16 [4, 1152, 128], P('segment'), may hold values from -2 to 2
- frame_mixing: float32 [6, 128], replicated, may hold values from 0.1 to 0.9
- step_embed: float32 [6, 128], replicated, may hold values from -3 to 3
Outputs:
- sampled_clips: bfloat16 [4, 2, 256, 128, 128], P('segment', None, 'tile')
The draws below stay inside these ranges and needn't reach their ends.
All inputs are finite; a program needn't handle non-finite values.
Results may differ from the reference program's by a relative error of at most 0.017.
Values may be sent and summed in bfloat16 or wider, within the bound.
A program may use at most 64 MiB of HBM per device.

```python
import math
import jax
import jax.numpy as jnp
from jax import lax

C = 128
FRAMES = 2
COLS = 128
STEPS_BASE = 3
STEPS_SR = 1
NSTEP = 6
MB = 4
ROWS = 256
N_SEGMENT = 4


def draw_section_weights(key, part):
    shape = (N_SEGMENT, 3, 3, C, C)
    base = jnp.clip(jax.random.normal(key, shape, jnp.float32), -3.5, 3.5)
    row_gain = jnp.array([1.0, 0.25, 0.6], jnp.float32)
    scaled = base * row_gain[None, :, None, None, None] * (4.0 / math.sqrt(3.0 * C))
    return scaled.reshape(N_SEGMENT, 9 * C, C).astype(jnp.bfloat16)


def block_levels(own_key, extent, cuts, smallest, largest):
    level, own = 1.0, jax.random.fold_in(own_key, 6)
    for position, blocks in cuts:
        heights = jnp.exp(jax.random.uniform(jax.random.fold_in(own, position), (blocks,), jnp.float32, smallest / len(cuts), largest / len(cuts)))
        level = level * jnp.repeat(heights, extent[position] // blocks).reshape([-1 if axis == position else 1 for axis in range(len(extent))])
    return level


def centred(rng, shape, width, reach, shards=(), dtype=jnp.bfloat16):
    loudness = block_levels(rng, shape, shards, -0.22, 0.18) if shards else 1.0
    values = jax.random.normal(rng, shape, jnp.float32) * width * loudness
    return jnp.minimum(jnp.maximum(values, -reach), reach).astype(dtype)


def setup_inputs(seed: int = 0) -> dict:
    key_of = jax.random.split(jax.random.key(seed), 6)
    latent_clips = centred(key_of[0], (MB, FRAMES, ROWS, COLS, C), 0.25, 1.5, ((0, 4), (2, 64)))
    augment_noise = centred(key_of[1], (N_SEGMENT, MB, FRAMES, ROWS, COLS, C), 0.6, 3.59375, ((0, 4), (3, 64)))
    section_weights = draw_section_weights(jax.random.fold_in(key_of[5], 71), 0)
    frame_mixing = jnp.clip(jax.random.uniform(key_of[3], (NSTEP, C), jnp.float32, 0.1, 0.9), 0.1, 0.9)
    step_embed = centred(key_of[4], (NSTEP, C), 0.5, 3.0, (), jnp.float32)
    return {"latent_clips": latent_clips, "augment_noise": augment_noise, "section_weights": section_weights, "frame_mixing": frame_mixing, "step_embed": step_embed}


norm_eps = 1e-06
keep_coef = 0.9
update_coef = 0.5
noise_coef = 0.5

def conv_step(latent, weight, mixing, embedding):
    latent_f32 = latent.astype(jnp.float32)
    frame_mean = lax.optimization_barrier(jnp.mean(latent_f32, axis=0, keepdims=True))
    mixed = (latent_f32 + mixing * (frame_mean - latent_f32)).astype(jnp.bfloat16)
    padded = jnp.pad(mixed, ((0, 0), (1, 1), (1, 1), (0, 0)))
    row_count = mixed.shape[1]
    col_count = mixed.shape[2]
    patches = jnp.concatenate([padded[:, row_off:row_off + row_count, col_off:col_off + col_count, :] for row_off in range(3) for col_off in range(3)], axis=-1)
    conv_out = jnp.dot(patches.reshape(-1, patches.shape[-1]), weight, preferred_element_type=jnp.float32).reshape(latent.shape) + embedding
    scaled = conv_out * lax.rsqrt(lax.optimization_barrier(jnp.mean(conv_out * conv_out, axis=-1, keepdims=True)) + norm_eps)
    return (keep_coef * latent_f32 + update_coef * jax.nn.silu(scaled)).astype(jnp.bfloat16)

def reference(latent_clips, augment_noise, section_weights, frame_mixing, step_embed):
    finished = []
    for clip_index in range(MB):
        latent = latent_clips[clip_index]
        step_index = 0
        for section in range(N_SEGMENT):
            latent = (latent.astype(jnp.float32) + noise_coef * augment_noise[section, clip_index].astype(jnp.float32)).astype(jnp.bfloat16)
            count = STEPS_BASE if section == 0 else STEPS_SR
            for repeat in range(count):
                latent = conv_step(latent, section_weights[section], frame_mixing[step_index], step_embed[step_index])
                step_index = step_index + 1
        finished.append(latent)
    return jnp.stack(finished)
```

```python
import functools

import jax
import jax.numpy as jnp
from jax import lax
from jax.experimental import pallas as pl
from jax.experimental.pallas import tpu as pltpu
from jax.sharding import PartitionSpec as P

MESH = pl.DeviceIdType.MESH
C = 128
COLS = 128
FRAMES = 2
STRIP = 4
HALO = 6
WIN = STRIP + 2 * HALO
NSEC = 4
NSTEP = 6
SECTION = (0, 0, 0, 1, 2, 3)
NEDGE = 3
NROWS = STRIP + 2 * NEDGE
SLICE = 9 * C // 8

norm_eps = 1e-06


def kernel(tiles, per_z, latent_ref, noise_ref, weight_ref, mix_ref, emb_ref, out_ref,
           aug, lat, mx, nz, wts,
           x_send, x_recv, wx_send, wx_recv, wz_send, wz_recv, wc_send, wc_recv,
           a_send, a_recv, n_send, n_recv, own_sem):
    me = lax.axis_index("segment")
    t = lax.axis_index("tile")
    core = lax.rem(t, 2)
    zq = lax.rem(t // per_z, 4)
    part = core * 4 + zq

    def tile_at(d):
        return lax.rem(t + d + tiles, tiles)

    def seg_at(d):
        return lax.rem(me + d, NSEC)

    def quad_at(d):
        return t + (lax.rem(zq + d, 4) - zq) * per_z

    partner = t + 1 - 2 * core

    own_noise = [
        pltpu.make_async_copy(
            noise_ref.at[0, me, :, pl.ds(2 * h, 2)],
            nz.at[me, :, pl.ds(NEDGE + 2 * h, 2)],
            x_recv.at[h, 0],
        )
        for h in range(2)
    ]
    own_weight = pltpu.make_async_copy(weight_ref.at[0], wts.at[me], own_sem)
    for c in own_noise:
        c.start()
    own_weight.start()

    barrier = pltpu.get_barrier_semaphore()
    others = [(seg_at(d), t) for d in (1, 2, 3)]
    others += [(me, quad_at(d)) for d in (1, 2, 3)]
    others += [(me, tile_at(d)) for d in (-2, -1, 1, 2)]
    for dev in others:
        pl.semaphore_signal(barrier, inc=1, device_id=dev, device_id_type=MESH)
    pl.semaphore_wait(barrier, len(others))

    rows_of = pl.ds(pl.multiple_of(part * SLICE, 16), SLICE)
    wx = {
        d: pltpu.make_async_remote_copy(
            src_ref=weight_ref.at[0, rows_of],
            dst_ref=wts.at[me, rows_of],
            send_sem=wx_send.at[d],
            recv_sem=wx_recv.at[d],
            device_id=(seg_at(d), t),
            device_id_type=MESH,
        )
        for d in (1, 2, 3)
    }
    nx = {
        (h, d): pltpu.make_async_remote_copy(
            src_ref=noise_ref.at[0, seg_at(d), :, pl.ds(2 * h, 2)],
            dst_ref=nz.at[me, :, pl.ds(NEDGE + 2 * h, 2)],
            send_sem=x_send.at[h, d],
            recv_sem=x_recv.at[h, d],
            device_id=(seg_at(d), t),
            device_id_type=MESH,
        )
        for d in (1, 2, 3)
        for h in range(2)
    }
    for d in (2, 1, 3):
        wx[d].start()
    even = lax.rem(me, 2) == 0
    for h in range(2):
        @pl.when(even)
        def _():
            nx[h, 2].start()
        nx[h, 1].start()
        nx[h, 3].start()

    wz = {}
    for j in (1, 2, 3):
        sec = lax.rem(me - j + NSEC, NSEC)
        for d in (1, 2, 3):
            wz[j, d] = pltpu.make_async_remote_copy(
                src_ref=wts.at[sec, rows_of],
                dst_ref=wts.at[sec, rows_of],
                send_sem=wz_send.at[j, d],
                recv_sem=wz_recv.at[j, d],
                device_id=(me, quad_at(d)),
                device_id_type=MESH,
            )
    for j in (1, 2, 3):
        wx[j].wait_recv()
        for d in (1, 2, 3):
            wz[j, d].start()

    def wait_noise(sec, h):
        piece = nz.at[sec, :, pl.ds(NEDGE + 2 * h, 2)]
        pltpu.make_async_copy(piece, piece, x_recv.at[h, lax.rem(me - sec + NSEC, NSEC)]).wait()

    def send_rows(i, row, count, to_row, d):
        return pltpu.make_async_remote_copy(
            src_ref=aug.at[pl.ds(HALO + row, count)],
            dst_ref=aug.at[pl.ds(to_row, count)],
            send_sem=a_send.at[i],
            recv_sem=a_recv.at[i],
            device_id=(me, tile_at(d)),
            device_id_type=MESH,
        )

    halo = [
        [send_rows(0, 0, 2, 10, -1), send_rows(1, 0, 2, 14, -2), send_rows(2, 0, 2, 2, 1)],
        [send_rows(3, 2, 2, 4, 1), send_rows(4, 2, 2, 0, 2), send_rows(5, 2, 2, 12, -1)],
    ]
    wc = {}
    for h in range(2):
        wait_noise(0, h)
        for row in (2 * h, 2 * h + 1):
            for f in range(FRAMES):
                aug[HALO + row, f] = (
                    latent_ref[0, f, row].astype(jnp.float32)
                    + 0.5 * nz[0, f, NEDGE + row].astype(jnp.float32)
                ).astype(jnp.bfloat16)
        for c in halo[h]:
            c.start()
        if h == 0:
            half = pl.ds(pl.multiple_of(core * 4 * SLICE, 16), 4 * SLICE)
            for j in (1, 2, 3):
                sec = lax.rem(me - j + NSEC, NSEC)
                for d in (1, 2, 3):
                    wz[j, d].wait_recv()
                wc[j] = pltpu.make_async_remote_copy(
                    src_ref=wts.at[sec, half],
                    dst_ref=wts.at[sec, half],
                    send_sem=wc_send.at[j],
                    recv_sem=wc_recv.at[j],
                    device_id=(me, partner),
                    device_id_type=MESH,
                )
                wc[j].start()

    @pl.when(jnp.logical_not(even))
    def _():
        for h in range(2):
            nx[h, 2].start()

    first = t * STRIP - HALO
    col = lax.broadcasted_iota(jnp.int32, (COLS, C), 0)
    left_edge = col == 0
    right_edge = col == COLS - 1

    def put_mixed(dst, row, k, pair):
        valid = jnp.logical_and(first + row >= 0, first + row < tiles * STRIP)
        mean = 0.5 * (pair[0] + pair[1])
        factor = mix_ref[k:k + 1, :]
        for f in range(FRAMES):
            mixed = pair[f] + factor * (mean - pair[f])
            mixed = jnp.where(valid, mixed, 0.0)
            mx[dst, 1, row, f] = mixed.astype(jnp.bfloat16)
            mx[dst, 0, row, f] = jnp.where(left_edge, 0.0, pltpu.roll(mixed, 1, 0)).astype(jnp.bfloat16)
            mx[dst, 2, row, f] = jnp.where(right_edge, 0.0, pltpu.roll(mixed, COLS - 1, 0)).astype(jnp.bfloat16)

    def mix_rows(lo, count):
        def body(i, _):
            row = lo + i
            put_mixed(0, row, 0, [aug[row, f].astype(jnp.float32) for f in range(FRAMES)])
            return 0
        lax.fori_loop(0, count, body, 0)

    mix_rows(HALO, STRIP)
    for i in (0, 2, 3, 5, 1, 4):
        halo[i // 3][i % 3].wait_recv()
    mix_rows(0, HALO)
    mix_rows(HALO + STRIP, HALO)

    own_weight.wait()
    for j in (1, 2, 3):
        wc[j].wait_recv()

    def step(k):
        sec = SECTION[k]
        src, dst = k % 2, (k + 1) % 2
        lat_in = aug if k == 0 else lat
        entering = k + 1 < NSTEP and SECTION[k + 1] != sec

        def body(p, _):
            base = k + 2 * p
            lhs = jnp.concatenate(
                [
                    mx[src, b, base + i].reshape(FRAMES * COLS, C)
                    for i in range(4)
                    for b in range(3)
                ],
                axis=1,
            )
            w = wts[sec]
            none = jnp.zeros((3 * C, C), jnp.bfloat16)
            rhs = jnp.concatenate(
                [jnp.concatenate([w, none], axis=0), jnp.concatenate([none, w], axis=0)], axis=1
            )
            acc = jnp.dot(lhs, rhs, preferred_element_type=jnp.float32)
            for j in range(2):
                row = base + 1 + j
                conv = acc[:, j * C:(j + 1) * C] + emb_ref[k:k + 1, :]
                power = jnp.mean(conv * conv, axis=-1, keepdims=True)
                half = conv * (0.5 * lax.rsqrt(power + norm_eps))
                silu = half + half * jnp.tanh(half)
                old = lat_in[row].reshape(FRAMES * COLS, C).astype(jnp.float32)
                new = (0.9 * old + 0.5 * silu).astype(jnp.bfloat16)
                if k == NSTEP - 1:
                    for f in range(FRAMES):
                        out_ref[0, f, row - HALO] = new[f * COLS:(f + 1) * COLS]
                    continue
                pair = [new[f * COLS:(f + 1) * COLS] for f in range(FRAMES)]
                if entering:
                    pair = [
                        (
                            v.astype(jnp.float32)
                            + 0.5 * nz[sec + 1, f, row - HALO + NEDGE].astype(jnp.float32)
                        ).astype(jnp.bfloat16)
                        for f, v in enumerate(pair)
                    ]
                for f in range(FRAMES):
                    lat[row, f] = pair[f]
                put_mixed(dst, row, k + 1, [v.astype(jnp.float32) for v in pair])
            return 0

        lax.fori_loop(0, (WIN - 2 * (k + 1)) // 2, body, 0)

    edge = {}

    def forward_noise(sec):
        count = NEDGE - (sec - 1)
        for h in range(2):
            wait_noise(sec, h)
        for i, (lo, to, d) in enumerate(
            ((NEDGE, NEDGE + STRIP, -1), (NEDGE + STRIP - count, NEDGE - count, 1))
        ):
            edge[sec, i] = pltpu.make_async_remote_copy(
                src_ref=nz.at[sec, :, pl.ds(lo, count)],
                dst_ref=nz.at[sec, :, pl.ds(to, count)],
                send_sem=n_send.at[sec - 1, i],
                recv_sem=n_recv.at[sec - 1, i],
                device_id=(me, tile_at(d)),
                device_id_type=MESH,
            )
            edge[sec, i].start()

    def wait_edge(sec):
        for i in range(2):
            edge[sec, i].wait_recv()

    step(0)
    forward_noise(1)
    step(1)
    forward_noise(2)
    forward_noise(3)
    wait_edge(1)
    step(2)
    wait_edge(2)
    step(3)
    wait_edge(3)
    step(4)
    step(5)

    for d in (1, 2, 3):
        wx[d].wait_send()
        wc[d].wait_send()
        for h in range(2):
            nx[h, d].wait_send()
        for e in (1, 2, 3):
            wz[d, e].wait_send()
        for i in range(2):
            edge[d, i].wait_send()
    for pieces in halo:
        for c in pieces:
            c.wait_send()


def build(mesh, per_z):
    tiles = mesh.shape["tile"]
    bf = jnp.bfloat16
    dma = pltpu.SemaphoreType.DMA

    def per_device(latent_clips, augment_noise, section_weights, frame_mixing, step_embed):
        vmem = pl.BlockSpec(memory_space=pltpu.VMEM)
        hbm = pl.BlockSpec(memory_space=pl.ANY)
        return pl.pallas_call(
            functools.partial(kernel, tiles, per_z),
            out_shape=jax.ShapeDtypeStruct(latent_clips.shape, bf),
            in_specs=[vmem, hbm, hbm, vmem, vmem],
            out_specs=vmem,
            scratch_shapes=[
                pltpu.VMEM((WIN, FRAMES, COLS, C), bf),
                pltpu.VMEM((WIN, FRAMES, COLS, C), bf),
                pltpu.VMEM((2, 3, WIN, FRAMES, COLS, C), bf),
                pltpu.VMEM((NSEC, FRAMES, NROWS, COLS, C), bf),
                pltpu.VMEM((NSEC, 9 * C, C), bf),
                dma((2, 4)), dma((2, 4)),
                dma((4,)), dma((4,)),
                dma((4, 4)), dma((4, 4)),
                dma((4,)), dma((4,)),
                dma((6,)), dma((6,)),
                dma((3, 2)), dma((3, 2)),
                dma,
            ],
            compiler_params=pltpu.CompilerParams(
                collective_id=0, has_side_effects=True, vmem_limit_bytes=48 << 20
            ),
        )(latent_clips, augment_noise, section_weights, frame_mixing, step_embed)

    return jax.shard_map(
        per_device,
        mesh=mesh,
        in_specs=(
            P("segment", None, "tile", None, None),
            P("segment", None, None, "tile", None, None),
            P("segment", None, None),
            P(),
            P(),
        ),
        out_specs=P("segment", None, "tile", None, None),
        check_vma=False,
    )


def solution(mesh):
    return build(mesh, 8)
```

```python
import functools

import jax
import jax.numpy as jnp
from jax import lax
from jax.experimental import pallas as pl
from jax.experimental.pallas import tpu as pltpu
from jax.sharding import PartitionSpec as P

MESH = pl.DeviceIdType.MESH
C = 128
COLS = 128
FRAMES = 2
STRIP = 4
HALO = 6
WIN = STRIP + 2 * HALO
NSEC = 4
NSTEP = 6
SECTION = (0, 0, 0, 1, 2, 3)
NEDGE = 3
NROWS = STRIP + 2 * NEDGE
SLICE = 9 * C // 8
GROUPS = {6: (3, 3), 5: (3, 2), 4: (4,), 3: (3,), 2: (2,)}
WIDEST = 4
ROW_ORDER = (0, 3, 1, 2)

norm_eps = 1e-06


def kernel(tiles, per_z, latent_hbm, noise_ref, weight_ref, mix_hbm, emb_hbm, out_ref,
           aug, lat, mxa, mxb, nz, wts, latent_ref, mix_ref, emb_ref, shift,
           f_send, f_recv, x_send, x_recv, wx_send, wx_recv, wz_send, wz_recv, wc_send, wc_recv,
           a_send, a_recv, n_send, n_recv, own_sem):
    me = lax.axis_index("segment")
    t = lax.axis_index("tile")
    core = lax.rem(t, 2)
    zq = lax.rem(t // per_z, 4)
    part = core * 4 + zq
    partner = t + 1 - 2 * core
    mx = (mxa, mxb)

    def tile_at(d):
        return lax.rem(t + d + tiles, tiles)

    def seg_at(d):
        return lax.rem(me + d, NSEC)

    def quad_at(d):
        return t + (lax.rem(zq + d, 4) - zq) * per_z

    def remote(src, dst, send, recv, seg, tile):
        return pltpu.make_async_remote_copy(
            src_ref=src,
            dst_ref=dst,
            send_sem=send,
            recv_sem=recv,
            device_id=(seg, tile),
            device_id_type=MESH,
        )

    def arrived(ref, sem):
        pltpu.make_async_copy(ref, ref, sem).wait()

    barrier = pltpu.get_barrier_semaphore()
    others = [(seg_at(d), t) for d in (1, 2, 3)]
    others += [(me, quad_at(d)) for d in (1, 2, 3)]
    others += [(me, tile_at(d)) for d in (-2, -1, 1, 2)]
    for dev in others:
        pl.semaphore_signal(barrier, inc=1, device_id=dev, device_id_type=MESH)

    def first_noise(row):
        return nz.at[0, :, pl.ds(NEDGE + row, 1)]

    def later_noise(sec):
        return nz.at[sec, :, pl.ds(NEDGE, STRIP)]

    own_weight = pltpu.make_async_copy(weight_ref.at[0], wts.at[me], own_sem.at[0])
    own_rest = [
        pltpu.make_async_copy(latent_hbm.at[0], latent_ref, own_sem.at[1]),
        pltpu.make_async_copy(mix_hbm, mix_ref, own_sem.at[2]),
        pltpu.make_async_copy(emb_hbm, emb_ref, own_sem.at[3]),
    ]
    for c in own_rest:
        c.start()

    @pl.when(me == 0)
    def _():
        for row in ROW_ORDER:
            pltpu.make_async_copy(
                noise_ref.at[0, me, :, pl.ds(row, 1)], first_noise(row), f_recv.at[row]
            ).start()

    @pl.when(me != 0)
    def _():
        pltpu.make_async_copy(noise_ref.at[0, me], later_noise(me), x_recv.at[me]).start()

    own_weight.start()
    for side in (0, COLS + 8):
        shift[:, pl.ds(side, 8)] = jnp.zeros((4 * WIDEST, 8, C), jnp.float32)
    pl.semaphore_wait(barrier, len(others))

    rows_of = pl.ds(pl.multiple_of(part * SLICE, 16), SLICE)
    half = pl.ds(pl.multiple_of(core * 4 * SLICE, 16), 4 * SLICE)

    def slice_to(d):
        return remote(weight_ref.at[0, rows_of], wts.at[me, rows_of],
                      wx_send.at[d], wx_recv.at[me], seg_at(d), t)

    def first_to(row, d):
        return remote(noise_ref.at[0, seg_at(d), :, pl.ds(row, 1)], first_noise(row),
                      f_send.at[row, d], f_recv.at[row], seg_at(d), t)

    def later_to(d):
        return remote(noise_ref.at[0, seg_at(d)], later_noise(me),
                      x_send.at[d], x_recv.at[me], seg_at(d), t)

    def gather(sec, d):
        return remote(wts.at[sec, rows_of], wts.at[sec, rows_of],
                      wz_send.at[sec, d], wz_recv.at[sec, d], me, quad_at(d))

    def share(sec):
        return remote(wts.at[sec, half], wts.at[sec, half],
                      wc_send.at[sec], wc_recv.at[sec], me, partner)

    for d in (2, 1, 3):
        slice_to(d).start()

    @pl.when(me == 0)
    def _():
        for row in ROW_ORDER:
            for d in (2, 1, 3):
                first_to(row, d).start()

    for sec, early in ((1, (3, 1)), (2, (2, 1, 3)), (3, (1, 3))):
        @pl.when(me == sec)
        def _(early=early):
            for d in early:
                later_to(d).start()

    def start_gather(sec):
        @pl.when(me != sec)
        def _():
            arrived(wts.at[sec, rows_of], wx_recv.at[sec])
            for d in (1, 2, 3):
                gather(sec, d).start()

    def start_share(sec):
        @pl.when(me != sec)
        def _():
            for d in (1, 2, 3):
                gather(sec, d).wait_recv()
            share(sec).start()

    def finish_share(sec):
        @pl.when(me != sec)
        def _():
            share(sec).wait_recv()

    start_gather(0)

    def row_copy(row, i):
        far = (14 + row, -2) if row < 2 else (row - 2, 2)
        to, d = ((10 + row, -1), (2 + row, 1), far)[i]
        return remote(aug.at[pl.ds(HALO + row, 1)], aug.at[pl.ds(to, 1)],
                      a_send.at[row, i], a_recv.at[row, i], me, tile_at(d))

    for c in own_rest:
        c.wait()
    for row in ROW_ORDER:
        arrived(first_noise(row), f_recv.at[row])
        for f in range(FRAMES):
            aug[HALO + row, f] = (
                latent_ref[f, row].astype(jnp.float32)
                + 0.5 * nz[0, f, NEDGE + row].astype(jnp.float32)
            ).astype(jnp.bfloat16)
        for i in range(3):
            row_copy(row, i).start()

    @pl.when(lax.rem(me, 2) == 1)
    def _():
        later_to(2).start()

    start_share(0)

    first = t * STRIP - HALO

    def put_mixed(dst, row, k, pair, slot):
        change = (0.5 * mix_ref[k:k + 1, :]) * (pair[1] - pair[0])
        for f, mixed in enumerate((pair[0] + change, pair[1] - change)):
            wide = shift.at[slot + f]
            wide[pl.ds(8, COLS)] = mixed
            mx[dst][1, row, f] = mixed.astype(jnp.bfloat16)
            mx[dst][0, row, f] = wide[pl.ds(7, COLS)].astype(jnp.bfloat16)
            mx[dst][2, row, f] = wide[pl.ds(9, COLS)].astype(jnp.bfloat16)

    def blank_outside(dst):
        zero = jnp.zeros((3, 1, FRAMES, COLS, C), jnp.bfloat16)

        def blank(row, _):
            mx[dst][:, pl.ds(row, 1)] = zero
            return 0

        @pl.when(first < 0)
        def _():
            lax.fori_loop(0, -first, blank, 0)

        @pl.when(first + WIN > tiles * STRIP)
        def _():
            lax.fori_loop(tiles * STRIP - first, WIN, blank, 0)

    def mix_rows(lo, count):
        def body(i, _):
            for j in range(2):
                row = lo + 2 * i + j
                put_mixed(0, row, 0, [aug[row, f].astype(jnp.float32) for f in range(FRAMES)], 2 * j)
            return 0
        lax.fori_loop(0, count // 2, body, 0)

    def step(k, bases=None):
        sec = SECTION[k]
        src, dst = k % 2, (k + 1) % 2
        lat_in = aug if k == 0 else lat
        entering = k + 1 < NSTEP and SECTION[k + 1] != sec

        def conv_of(base):
            lhs = jnp.concatenate(
                [
                    mx[src][b, base + i].reshape(FRAMES * COLS, C)
                    for i in range(4)
                    for b in range(3)
                ],
                axis=1,
            )
            w = wts[sec]
            none = jnp.zeros((3 * C, C), jnp.bfloat16)
            rhs = jnp.concatenate(
                [jnp.concatenate([w, none], axis=0), jnp.concatenate([none, w], axis=0)], axis=1
            )
            return jnp.dot(lhs, rhs, preferred_element_type=jnp.float32)

        def finish(base, acc, slot):
            for j in range(2):
                row = base + 1 + j
                conv = acc[:, j * C:(j + 1) * C] + emb_ref[k:k + 1, :]
                power = jnp.sum(conv * conv, axis=-1, keepdims=True)
                half = conv * lax.rsqrt(power * (4.0 / C) + 4.0 * norm_eps)
                old = lat_in[row].reshape(FRAMES * COLS, C).astype(jnp.float32)
                new = (0.9 * old + (0.5 * half) * (1.0 + jnp.tanh(half))).astype(jnp.bfloat16)
                if k == NSTEP - 1:
                    for f in range(FRAMES):
                        out_ref[0, f, row - HALO] = new[f * COLS:(f + 1) * COLS]
                    continue
                pair = [new[f * COLS:(f + 1) * COLS] for f in range(FRAMES)]
                if entering:
                    pair = [
                        (
                            v.astype(jnp.float32)
                            + 0.5 * nz[sec + 1, f, row - HALO + NEDGE].astype(jnp.float32)
                        ).astype(jnp.bfloat16)
                        for f, v in enumerate(pair)
                    ]
                for f in range(FRAMES):
                    lat[row, f] = pair[f]
                put_mixed(dst, row, k + 1, [v.astype(jnp.float32) for v in pair], slot + 2 * j)

        def several(bases):
            accs = [conv_of(base) for base in bases]
            for i, base in enumerate(bases):
                finish(base, accs[i], 4 * i)

        def run(lo, groups):
            times = len(groups) if len(set(groups)) == 1 else 1
            if times == 1:
                for take in groups:
                    several([lo + 2 * i for i in range(take)])
                    lo += 2 * take
                return
            take = groups[0]

            def body(p, _):
                several([lo + 2 * (p * take + i) for i in range(take)])
                return 0

            lax.fori_loop(0, times, body, 0)

        if bases is not None:
            several(bases)
        else:
            run(k, GROUPS[(WIN - 2 * (k + 1)) // 2])
        if k < NSTEP - 1 and bases is None:
            blank_outside(dst)

    edge = {}

    def forward_noise(sec):
        count = NEDGE - (sec - 1)
        arrived(later_noise(sec), x_recv.at[sec])
        for i, (lo, to, d) in enumerate(
            ((NEDGE, NEDGE + STRIP, -1), (NEDGE + STRIP - count, NEDGE - count, 1))
        ):
            edge[sec, i] = remote(
                nz.at[sec, :, pl.ds(lo, count)], nz.at[sec, :, pl.ds(to, count)],
                n_send.at[sec - 1, i], n_recv.at[sec - 1, i], me, tile_at(d),
            )
            edge[sec, i].start()

    def wait_edge(sec):
        for i in range(2):
            edge[sec, i].wait_recv()

    chip = HALO - STRIP * core
    mix_rows(HALO, STRIP)
    near = (HALO + STRIP) - 2 * STRIP * core
    for row in range(STRIP):
        arrived(aug.at[pl.ds(near + row, 1)], a_recv.at[row, core])
    mix_rows(near, STRIP)
    own_weight.wait()
    finish_share(0)
    step(0, [chip + 2 * i for i in range(3)])
    for sec in (1, 2, 3):
        start_gather(sec)
    over = (HALO - STRIP) + 2 * STRIP * core
    for row in range(STRIP):
        arrived(aug.at[pl.ds(over + row, 1)], a_recv.at[row, 1 - core])
    mix_rows(over, STRIP)
    for row in range(STRIP):
        row_copy(row, 2).wait_recv()
    mix_rows(0, 2)
    mix_rows(WIN - 2, 2)
    blank_outside(0)
    step(0, [lax.rem(chip + 6 + 2 * i, 14) for i in range(4)])
    blank_outside(1)
    forward_noise(1)
    step(1)
    for sec in (1, 2, 3):
        start_share(sec)
    forward_noise(2)
    forward_noise(3)
    wait_edge(1)
    step(2)
    finish_share(1)
    wait_edge(2)
    step(3)
    finish_share(2)
    wait_edge(3)
    step(4)
    finish_share(3)
    step(5)

    for d in (1, 2, 3):
        slice_to(d).wait_send()
        for i in range(2):
            edge[d, i].wait_send()

    @pl.when(me == 0)
    def _():
        for row in ROW_ORDER:
            for d in (1, 2, 3):
                first_to(row, d).wait_send()

    @pl.when(me != 0)
    def _():
        for d in (1, 2, 3):
            later_to(d).wait_send()

    for sec in range(NSEC):
        @pl.when(me != sec)
        def _(sec=sec):
            for d in (1, 2, 3):
                gather(sec, d).wait_send()
            share(sec).wait_send()

    for row in range(STRIP):
        for i in range(3):
            row_copy(row, i).wait_send()


def build(mesh, per_z):
    tiles = mesh.shape["tile"]
    bf = jnp.bfloat16
    dma = pltpu.SemaphoreType.DMA

    def per_device(latent_clips, augment_noise, section_weights, frame_mixing, step_embed):
        vmem = pl.BlockSpec(memory_space=pltpu.VMEM)
        hbm = pl.BlockSpec(memory_space=pltpu.HBM)
        return pl.pallas_call(
            functools.partial(kernel, tiles, per_z),
            out_shape=jax.ShapeDtypeStruct(latent_clips.shape, bf),
            in_specs=[hbm, hbm, hbm, hbm, hbm],
            out_specs=vmem,
            scratch_shapes=[
                pltpu.VMEM((WIN, FRAMES, COLS, C), bf),
                pltpu.VMEM((WIN, FRAMES, COLS, C), bf),
                pltpu.VMEM((3, WIN, FRAMES, COLS, C), bf),
                pltpu.VMEM((3, WIN, FRAMES, COLS, C), bf),
                pltpu.VMEM((NSEC, FRAMES, NROWS, COLS, C), bf),
                pltpu.VMEM((NSEC, 9 * C, C), bf),
                pltpu.VMEM((FRAMES, STRIP, COLS, C), bf),
                pltpu.VMEM((NSTEP, C), jnp.float32),
                pltpu.VMEM((NSTEP, C), jnp.float32),
                pltpu.VMEM((4 * WIDEST, COLS + 16, C), jnp.float32),
                dma((STRIP, 4)), dma((STRIP,)),
                dma((4,)), dma((NSEC,)),
                dma((4,)), dma((NSEC,)),
                dma((NSEC, 4)), dma((NSEC, 4)),
                dma((NSEC,)), dma((NSEC,)),
                dma((STRIP, 3)), dma((STRIP, 3)),
                dma((3, 2)), dma((3, 2)),
                dma((4,)),
            ],
            compiler_params=pltpu.CompilerParams(
                collective_id=0, has_side_effects=True, vmem_limit_bytes=61 << 20
            ),
        )(latent_clips, augment_noise, section_weights, frame_mixing, step_embed)

    return jax.shard_map(
        per_device,
        mesh=mesh,
        in_specs=(
            P("segment", None, "tile", None, None),
            P("segment", None, None, "tile", None, None),
            P("segment", None, None),
            P(),
            P(),
        ),
        out_specs=P("segment", None, "tile", None, None),
        check_vma=False,
    )


def solution(mesh):
    return build(mesh, 8)
```

```python
import functools

import jax
import jax.numpy as jnp
from jax import lax
from jax.experimental import pallas as pl
from jax.experimental.pallas import tpu as pltpu
from jax.sharding import PartitionSpec as P

MESH = pl.DeviceIdType.MESH
C = 128
COLS = 128
FRAMES = 2
STRIP = 4
HALO = 3
WIN = STRIP + 2 * HALO
NSEC = 4
NSTEP = 6
SECTION = (0, 0, 0, 1, 2, 3)
NEDGE = 2
NROWS = STRIP + 2 * NEDGE
SLICE = 9 * C // 8
SHIFTS = 12
ROW_ORDER = (1, 2, 0, 3)

norm_eps = 1e-06


def kernel(tiles, per_z, latent_hbm, noise_ref, weight_ref, mix_hbm, emb_hbm, out_ref,
           entry, lat, mxa, mxb, nz, wts, latent_ref, mix_ref, emb_ref, shift,
           f_send, f_recv, x_send, x_recv, wx_send, wx_recv, wz_send, wz_recv, wc_send, wc_recv,
           a_send, a_recv, b_send, b_recv, n_send, n_recv, own_sem):
    me = lax.axis_index("segment")
    t = lax.axis_index("tile")
    core = lax.rem(t, 2)
    zq = lax.rem(t // per_z, 4)
    part = core * 4 + zq
    partner = t + 1 - 2 * core
    mx = (mxa, mxb)

    def tile_at(d):
        return lax.rem(t + d + tiles, tiles)

    def seg_at(d):
        return lax.rem(me + d, NSEC)

    def quad_at(d):
        return t + (lax.rem(zq + d, 4) - zq) * per_z

    def remote(src, dst, send, recv, seg, tile):
        return pltpu.make_async_remote_copy(
            src_ref=src,
            dst_ref=dst,
            send_sem=send,
            recv_sem=recv,
            device_id=(seg, tile),
            device_id_type=MESH,
        )

    def arrived(ref, sem):
        pltpu.make_async_copy(ref, ref, sem).wait()

    barrier = pltpu.get_barrier_semaphore()
    others = [(seg_at(d), t) for d in (1, 2, 3)]
    others += [(me, quad_at(d)) for d in (1, 2, 3)]
    others += [(me, tile_at(d)) for d in (-1, 1)]
    for dev in others:
        pl.semaphore_signal(barrier, inc=1, device_id=dev, device_id_type=MESH)

    def first_noise(row):
        return nz.at[0, :, pl.ds(NEDGE + row, 1)]

    def later_noise(sec):
        return nz.at[sec, :, pl.ds(NEDGE, STRIP)]

    own_weight = pltpu.make_async_copy(weight_ref.at[0], wts.at[me], own_sem.at[0])
    own_rest = [
        pltpu.make_async_copy(latent_hbm.at[0], latent_ref, own_sem.at[1]),
        pltpu.make_async_copy(mix_hbm, mix_ref, own_sem.at[2]),
        pltpu.make_async_copy(emb_hbm, emb_ref, own_sem.at[3]),
    ]
    for c in own_rest:
        c.start()

    @pl.when(me == 0)
    def _():
        for row in ROW_ORDER:
            pltpu.make_async_copy(
                noise_ref.at[0, me, :, pl.ds(row, 1)], first_noise(row), f_recv.at[row]
            ).start()

    @pl.when(me != 0)
    def _():
        pltpu.make_async_copy(noise_ref.at[0, me], later_noise(me), x_recv.at[me]).start()

    own_weight.start()
    for side in (0, COLS + 8):
        shift[:, pl.ds(side, 8)] = jnp.zeros((SHIFTS, 8, C), jnp.float32)
    pl.semaphore_wait(barrier, len(others))

    rows_of = pl.ds(pl.multiple_of(part * SLICE, 16), SLICE)
    half = pl.ds(pl.multiple_of(core * 4 * SLICE, 16), 4 * SLICE)

    def slice_to(d):
        return remote(weight_ref.at[0, rows_of], wts.at[me, rows_of],
                      wx_send.at[d], wx_recv.at[me], seg_at(d), t)

    def first_to(row, d):
        return remote(noise_ref.at[0, seg_at(d), :, pl.ds(row, 1)], first_noise(row),
                      f_send.at[row, d], f_recv.at[row], seg_at(d), t)

    def later_to(d):
        return remote(noise_ref.at[0, seg_at(d)], later_noise(me),
                      x_send.at[d], x_recv.at[me], seg_at(d), t)

    def gather(sec, d):
        return remote(wts.at[sec, rows_of], wts.at[sec, rows_of],
                      wz_send.at[sec, d], wz_recv.at[sec, d], me, quad_at(d))

    def share(sec):
        return remote(wts.at[sec, half], wts.at[sec, half],
                      wc_send.at[sec], wc_recv.at[sec], me, partner)

    for d in (2, 1, 3):
        slice_to(d).start()

    @pl.when(me == 0)
    def _():
        for row in ROW_ORDER:
            for d in (2, 1, 3):
                first_to(row, d).start()

    for sec, early in ((1, (3, 2, 1)), (2, (2, 1, 3)), (3, (1, 3, 2))):
        @pl.when(me == sec)
        def _(early=early):
            for d in early:
                later_to(d).start()

    def start_gather(sec):
        @pl.when(me != sec)
        def _():
            arrived(wts.at[sec, rows_of], wx_recv.at[sec])
            for d in (1, 2, 3):
                gather(sec, d).start()

    def start_share(sec):
        @pl.when(me != sec)
        def _():
            for d in (1, 2, 3):
                gather(sec, d).wait_recv()
            share(sec).start()

    def finish_share(sec):
        @pl.when(me != sec)
        def _():
            share(sec).wait_recv()

    for sec in range(NSEC):
        start_gather(sec)

    def row_copy(row, i):
        to, d = ((HALO + STRIP + row, -1), (row - 1, 1))[i]
        return remote(entry.at[0, pl.ds(HALO + row, 1)], entry.at[0, pl.ds(to, 1)],
                      a_send.at[row, i], a_recv.at[row, i], me, tile_at(d))

    def goes(row):
        return [i for i in range(2) if 0 <= row - i < HALO]

    def strip_copy(i):
        lo, to, d = ((HALO, HALO + STRIP, -1), (HALO + 1, 0, 1))[i]
        return remote(entry.at[1, pl.ds(lo, HALO)], entry.at[1, pl.ds(to, HALO)],
                      b_send.at[i], b_recv.at[i], me, tile_at(d))

    for c in own_rest:
        c.wait()
    for row in ROW_ORDER:
        arrived(first_noise(row), f_recv.at[row])
        for f in range(FRAMES):
            entry[0, HALO + row, f] = (
                latent_ref[f, row].astype(jnp.float32)
                + 0.5 * nz[0, f, NEDGE + row].astype(jnp.float32)
            ).astype(jnp.bfloat16)
        for i in goes(row):
            row_copy(row, i).start()

    start_share(0)

    def put_mixed(dst, row, k, pair, slot):
        change = (0.5 * mix_ref[k:k + 1, :]) * (pair[1] - pair[0])
        for f, mixed in enumerate((pair[0] + change, pair[1] - change)):
            wide = shift.at[slot + f]
            wide[pl.ds(8, COLS)] = mixed
            mx[dst][1, row, f] = mixed.astype(jnp.bfloat16)
            mx[dst][0, row, f] = wide[pl.ds(7, COLS)].astype(jnp.bfloat16)
            mx[dst][2, row, f] = wide[pl.ds(9, COLS)].astype(jnp.bfloat16)

    def blank_outside(dst):
        zero = jnp.zeros((3, HALO, FRAMES, COLS, C), jnp.bfloat16)

        @pl.when(t == 0)
        def _():
            mx[dst][:, pl.ds(0, HALO)] = zero

        @pl.when(t == tiles - 1)
        def _():
            mx[dst][:, pl.ds(HALO + STRIP, HALO)] = zero

    def mix_rows(k, lo, count):
        for j in range(count):
            put_mixed(
                k % 2, lo + j, k,
                [entry[k // 3, lo + j, f].astype(jnp.float32) for f in range(FRAMES)], 2 * j,
            )

    def step(k, bases=None):
        sec = SECTION[k]
        src, dst = k % 2, (k + 1) % 2
        lat_in = entry.at[k // 3] if k % 3 == 0 else lat
        lat_out = entry.at[1] if k == 2 else lat
        entering = k + 1 < NSTEP and SECTION[k + 1] != sec

        def conv_of(base):
            lhs = jnp.concatenate(
                [
                    mx[src][b, base + i].reshape(FRAMES * COLS, C)
                    for i in range(4)
                    for b in range(3)
                ],
                axis=1,
            )
            w = wts[sec]
            none = jnp.zeros((3 * C, C), jnp.bfloat16)
            rhs = jnp.concatenate(
                [jnp.concatenate([w, none], axis=0), jnp.concatenate([none, w], axis=0)], axis=1
            )
            return jnp.dot(lhs, rhs, preferred_element_type=jnp.float32)

        def finish(base, acc, slot):
            for j in range(2):
                row = base + 1 + j
                conv = acc[:, j * C:(j + 1) * C] + emb_ref[k:k + 1, :]
                power = jnp.sum(conv * conv, axis=-1, keepdims=True)
                half = conv * lax.rsqrt(power * (4.0 / C) + 4.0 * norm_eps)
                old = lat_in[row].reshape(FRAMES * COLS, C).astype(jnp.float32)
                new = (0.9 * old + (0.5 * half) * (1.0 + jnp.tanh(half))).astype(jnp.bfloat16)
                if k == NSTEP - 1:
                    for f in range(FRAMES):
                        out_ref[0, f, row - HALO] = new[f * COLS:(f + 1) * COLS]
                    continue
                pair = [new[f * COLS:(f + 1) * COLS] for f in range(FRAMES)]
                if entering:
                    pair = [
                        (
                            v.astype(jnp.float32)
                            + 0.5 * nz[sec + 1, f, row - HALO + NEDGE].astype(jnp.float32)
                        ).astype(jnp.bfloat16)
                        for f, v in enumerate(pair)
                    ]
                for f in range(FRAMES):
                    lat_out[row, f] = pair[f]
                put_mixed(dst, row, k + 1, [v.astype(jnp.float32) for v in pair], slot + 2 * j)

        def several(bases):
            accs = [conv_of(base) for base in bases]
            for i, base in enumerate(bases):
                finish(base, accs[i], 4 * i)

        if bases is None:
            several([k % 3 + 2 * i for i in range(4 - k % 3)])
        else:
            several(bases)

    def edge_copy(sec, i):
        count = NSEC - sec
        lo, to, d = (
            (NEDGE, NEDGE + STRIP, -1),
            (NEDGE + STRIP - count, NEDGE - count, 1),
        )[i]
        return remote(nz.at[sec, :, pl.ds(lo, count)], nz.at[sec, :, pl.ds(to, count)],
                      n_send.at[sec, i], n_recv.at[sec, i], me, tile_at(d))

    def forward_noise(sec):
        arrived(later_noise(sec), x_recv.at[sec])
        for i in range(2):
            edge_copy(sec, i).start()

    def wait_edge(sec):
        for i in range(2):
            edge_copy(sec, i).wait_recv()

    near = (HALO + STRIP) * (1 - core)
    over = (HALO + STRIP) * core
    inner = (1 - core) * STRIP
    outer = core * STRIP

    mix_rows(0, HALO, STRIP)
    for row in range(HALO):
        arrived(entry.at[0, pl.ds(near + row, 1)], a_recv.at[row + core, core])
    mix_rows(0, near, HALO)
    own_weight.wait()
    finish_share(0)
    step(0, [inner, inner + 2])
    for row in range(HALO):
        arrived(entry.at[0, pl.ds(over + row, 1)], a_recv.at[row + 1 - core, 1 - core])
    mix_rows(0, over, HALO)
    blank_outside(0)
    step(0, [outer, outer + 2])
    blank_outside(1)
    forward_noise(2)
    forward_noise(3)
    step(1)
    blank_outside(0)
    arrived(later_noise(1), x_recv.at[1])
    step(2)
    for i in range(2):
        strip_copy(i).start()

    for sec in (1, 2, 3):
        start_share(sec)
    arrived(entry.at[1, pl.ds(near, HALO)], b_recv.at[core])
    mix_rows(3, near, HALO)
    finish_share(1)
    wait_edge(2)
    step(3, [inner, inner + 2])
    arrived(entry.at[1, pl.ds(over, HALO)], b_recv.at[1 - core])
    mix_rows(3, over, HALO)
    blank_outside(1)
    step(3, [outer, outer + 2])
    blank_outside(0)
    finish_share(2)
    wait_edge(3)
    step(4)
    blank_outside(1)
    finish_share(3)
    step(5)

    for d in (1, 2, 3):
        slice_to(d).wait_send()
    for i in range(2):
        strip_copy(i).wait_send()
        for sec in (2, 3):
            edge_copy(sec, i).wait_send()

    @pl.when(me == 0)
    def _():
        for row in ROW_ORDER:
            for d in (1, 2, 3):
                first_to(row, d).wait_send()

    @pl.when(me != 0)
    def _():
        for d in (1, 2, 3):
            later_to(d).wait_send()

    for sec in range(NSEC):
        @pl.when(me != sec)
        def _(sec=sec):
            for d in (1, 2, 3):
                gather(sec, d).wait_send()
            share(sec).wait_send()

    for row in range(STRIP):
        for i in goes(row):
            row_copy(row, i).wait_send()


def build(mesh, per_z):
    tiles = mesh.shape["tile"]
    bf = jnp.bfloat16
    dma = pltpu.SemaphoreType.DMA

    def per_device(latent_clips, augment_noise, section_weights, frame_mixing, step_embed):
        vmem = pl.BlockSpec(memory_space=pltpu.VMEM)
        hbm = pl.BlockSpec(memory_space=pltpu.HBM)
        return pl.pallas_call(
            functools.partial(kernel, tiles, per_z),
            out_shape=jax.ShapeDtypeStruct(latent_clips.shape, bf),
            in_specs=[hbm, hbm, hbm, hbm, hbm],
            out_specs=vmem,
            scratch_shapes=[
                pltpu.VMEM((2, WIN, FRAMES, COLS, C), bf),
                pltpu.VMEM((WIN, FRAMES, COLS, C), bf),
                pltpu.VMEM((3, WIN, FRAMES, COLS, C), bf),
                pltpu.VMEM((3, WIN, FRAMES, COLS, C), bf),
                pltpu.VMEM((NSEC, FRAMES, NROWS, COLS, C), bf),
                pltpu.VMEM((NSEC, 9 * C, C), bf),
                pltpu.VMEM((FRAMES, STRIP, COLS, C), bf),
                pltpu.VMEM((NSTEP, C), jnp.float32),
                pltpu.VMEM((NSTEP, C), jnp.float32),
                pltpu.VMEM((SHIFTS, COLS + 16, C), jnp.float32),
                dma((STRIP, 4)), dma((STRIP,)),
                dma((4,)), dma((NSEC,)),
                dma((4,)), dma((NSEC,)),
                dma((NSEC, 4)), dma((NSEC, 4)),
                dma((NSEC,)), dma((NSEC,)),
                dma((STRIP, 2)), dma((STRIP, 2)),
                dma((2,)), dma((2,)),
                dma((NSEC, 2)), dma((NSEC, 2)),
                dma((4,)),
            ],
            compiler_params=pltpu.CompilerParams(
                collective_id=0, has_side_effects=True, vmem_limit_bytes=61 << 20
            ),
        )(latent_clips, augment_noise, section_weights, frame_mixing, step_embed)

    return jax.shard_map(
        per_device,
        mesh=mesh,
        in_specs=(
            P("segment", None, "tile", None, None),
            P("segment", None, None, "tile", None, None),
            P("segment", None, None),
            P(),
            P(),
        ),
        out_specs=P("segment", None, "tile", None, None),
        check_vma=False,
    )


def solution(mesh):
    return build(mesh, 8)
```

```python
import functools

import jax
import jax.numpy as jnp
from jax import lax
from jax.experimental import pallas as pl
from jax.experimental.pallas import tpu as pltpu
from jax.sharding import PartitionSpec as P

MESH = pl.DeviceIdType.MESH
C = 128
COLS = 128
FRAMES = 2
STRIP = 4
HALO = 3
WIN = STRIP + 2 * HALO
NSEC = 4
NSTEP = 6
SECTION = (0, 0, 0, 1, 2, 3)
NEDGE = 2
NROWS = STRIP + 2 * NEDGE
SLICE = 9 * C // 8
SHIFTS = 12
ROW_ORDER = (1, 2, 0, 3)

norm_eps = 1e-06


def kernel(tiles, per_z, latent_hbm, noise_ref, weight_ref, mix_hbm, emb_hbm, out_ref,
           entry, lat, mxa, mxb, nz, wts, latent_ref, mix_ref, emb_ref, shift,
           f_send, f_recv, x_send, x_recv, wx_send, wx_recv, wz_send, wz_recv, wc_send, wc_recv,
           a_send, a_recv, b_send, b_recv, n_send, n_recv, own_sem):
    me = lax.axis_index("segment")
    t = lax.axis_index("tile")
    core = lax.rem(t, 2)
    zq = lax.rem(t // per_z, 4)
    part = core * 4 + zq
    partner = t + 1 - 2 * core
    mx = (mxa, mxb)

    def tile_at(d):
        return lax.rem(t + d + tiles, tiles)

    def seg_at(d):
        return lax.rem(me + d, NSEC)

    def quad_at(d):
        return t + (lax.rem(zq + d, 4) - zq) * per_z

    def remote(src, dst, send, recv, seg, tile):
        return pltpu.make_async_remote_copy(
            src_ref=src,
            dst_ref=dst,
            send_sem=send,
            recv_sem=recv,
            device_id=(seg, tile),
            device_id_type=MESH,
        )

    def arrived(ref, sem):
        pltpu.make_async_copy(ref, ref, sem).wait()

    barrier = pltpu.get_barrier_semaphore()
    others = [(seg_at(d), t) for d in (1, 2, 3)]
    others += [(me, quad_at(d)) for d in (1, 2, 3)]
    others += [(me, tile_at(d)) for d in (-1, 1)]
    for dev in others:
        pl.semaphore_signal(barrier, inc=1, device_id=dev, device_id_type=MESH)

    def first_noise(row):
        return nz.at[0, :, pl.ds(NEDGE + row, 1)]

    def later_noise(sec):
        return nz.at[sec, :, pl.ds(NEDGE, STRIP)]

    own_weight = pltpu.make_async_copy(weight_ref.at[0], wts.at[me], own_sem.at[0])
    own_rest = [
        pltpu.make_async_copy(latent_hbm.at[0], latent_ref, own_sem.at[1]),
        pltpu.make_async_copy(mix_hbm, mix_ref, own_sem.at[2]),
        pltpu.make_async_copy(emb_hbm, emb_ref, own_sem.at[3]),
    ]
    for c in own_rest:
        c.start()

    @pl.when(me == 0)
    def _():
        for row in ROW_ORDER:
            pltpu.make_async_copy(
                noise_ref.at[0, me, :, pl.ds(row, 1)], first_noise(row), f_recv.at[row]
            ).start()

    @pl.when(me != 0)
    def _():
        pltpu.make_async_copy(noise_ref.at[0, me], later_noise(me), x_recv.at[me]).start()

    own_weight.start()
    for side in (0, COLS + 8):
        shift[:, pl.ds(side, 8)] = jnp.zeros((SHIFTS, 8, C), jnp.float32)
    pl.semaphore_wait(barrier, len(others))

    rows_of = pl.ds(pl.multiple_of(part * SLICE, 16), SLICE)
    half = pl.ds(pl.multiple_of(core * 4 * SLICE, 16), 4 * SLICE)

    def slice_to(d):
        return remote(weight_ref.at[0, rows_of], wts.at[me, rows_of],
                      wx_send.at[d], wx_recv.at[me], seg_at(d), t)

    def first_to(row, d):
        return remote(noise_ref.at[0, seg_at(d), :, pl.ds(row, 1)], first_noise(row),
                      f_send.at[row, d], f_recv.at[row], seg_at(d), t)

    def later_to(d):
        return remote(noise_ref.at[0, seg_at(d)], later_noise(me),
                      x_send.at[d], x_recv.at[me], seg_at(d), t)

    def gather(sec, d):
        return remote(wts.at[sec, rows_of], wts.at[sec, rows_of],
                      wz_send.at[sec, d], wz_recv.at[sec, d], me, quad_at(d))

    def share(sec):
        return remote(wts.at[sec, half], wts.at[sec, half],
                      wc_send.at[sec], wc_recv.at[sec], me, partner)

    for d in (2, 1, 3):
        slice_to(d).start()

    @pl.when(me == 0)
    def _():
        for row in ROW_ORDER:
            for d in (2, 1, 3):
                first_to(row, d).start()

    for sec, early in ((1, (3, 2, 1)), (2, (2, 1, 3)), (3, (1, 3, 2))):
        @pl.when(me == sec)
        def _(early=early):
            for d in early:
                later_to(d).start()

    def start_gather(sec):
        @pl.when(me != sec)
        def _():
            arrived(wts.at[sec, rows_of], wx_recv.at[sec])
            for d in (1, 2, 3):
                gather(sec, d).start()

    def start_share(sec):
        @pl.when(me != sec)
        def _():
            for d in (1, 2, 3):
                gather(sec, d).wait_recv()
            share(sec).start()

    def finish_share(sec):
        @pl.when(me != sec)
        def _():
            share(sec).wait_recv()

    for sec in range(NSEC):
        start_gather(sec)

    def row_copy(row, i):
        to, d = ((HALO + STRIP + row, -1), (row - 1, 1))[i]
        return remote(entry.at[0, pl.ds(HALO + row, 1)], entry.at[0, pl.ds(to, 1)],
                      a_send.at[row, i], a_recv.at[row, i], me, tile_at(d))

    def goes(row):
        return [i for i in range(2) if 0 <= row - i < HALO]

    def strip_copy(i):
        lo, to, d = ((HALO, HALO + STRIP, -1), (HALO + 1, 0, 1))[i]
        return remote(entry.at[1, pl.ds(lo, HALO)], entry.at[1, pl.ds(to, HALO)],
                      b_send.at[i], b_recv.at[i], me, tile_at(d))

    for c in own_rest:
        c.wait()
    for row in ROW_ORDER:
        arrived(first_noise(row), f_recv.at[row])
        for f in range(FRAMES):
            entry[0, HALO + row, f] = (
                latent_ref[f, row].astype(jnp.float32)
                + 0.5 * nz[0, f, NEDGE + row].astype(jnp.float32)
            ).astype(jnp.bfloat16)
        for i in goes(row):
            row_copy(row, i).start()

    start_share(0)

    def put_mixed(dst, row, k, pair, slot):
        change = (0.5 * mix_ref[k:k + 1, :]) * (pair[1] - pair[0])
        for f, mixed in enumerate((pair[0] + change, pair[1] - change)):
            wide = shift.at[slot + f]
            wide[pl.ds(8, COLS)] = mixed
            mx[dst][1, row, f] = mixed.astype(jnp.bfloat16)
            mx[dst][0, row, f] = wide[pl.ds(7, COLS)].astype(jnp.bfloat16)
            mx[dst][2, row, f] = wide[pl.ds(9, COLS)].astype(jnp.bfloat16)

    def blank_outside(dst):
        zero = jnp.zeros((3, HALO, FRAMES, COLS, C), jnp.bfloat16)

        @pl.when(t == 0)
        def _():
            mx[dst][:, pl.ds(0, HALO)] = zero

        @pl.when(t == tiles - 1)
        def _():
            mx[dst][:, pl.ds(HALO + STRIP, HALO)] = zero

    def mix_rows(k, lo, count):
        for j in range(count):
            put_mixed(
                k % 2, lo + j, k,
                [entry[k // 3, lo + j, f].astype(jnp.float32) for f in range(FRAMES)], 2 * j,
            )

    def step(k, bases=None):
        sec = SECTION[k]
        src, dst = k % 2, (k + 1) % 2
        lat_in = entry.at[k // 3] if k % 3 == 0 else lat
        lat_out = entry.at[1] if k == 2 else lat
        entering = k + 1 < NSTEP and SECTION[k + 1] != sec

        def conv_of(base):
            lhs = jnp.concatenate(
                [
                    mx[src][b, base + i].reshape(FRAMES * COLS, C)
                    for i in range(4)
                    for b in range(3)
                ],
                axis=1,
            )
            w = wts[sec]
            none = jnp.zeros((3 * C, C), jnp.bfloat16)
            rhs = jnp.concatenate(
                [jnp.concatenate([w, none], axis=0), jnp.concatenate([none, w], axis=0)], axis=1
            )
            return jnp.dot(lhs, rhs, preferred_element_type=jnp.float32)

        def finish(base, acc, slot):
            for j in range(2):
                row = base + 1 + j
                conv = acc[:, j * C:(j + 1) * C] + emb_ref[k:k + 1, :]
                power = jnp.sum(conv * conv, axis=-1, keepdims=True)
                half = conv * lax.rsqrt(power * (4.0 / C) + 4.0 * norm_eps)
                old = lat_in[row].reshape(FRAMES * COLS, C).astype(jnp.float32)
                new = (0.9 * old + (0.5 * half) * (1.0 + jnp.tanh(half))).astype(jnp.bfloat16)
                if k == NSTEP - 1:
                    for f in range(FRAMES):
                        out_ref[0, f, row - HALO] = new[f * COLS:(f + 1) * COLS]
                    continue
                pair = [new[f * COLS:(f + 1) * COLS] for f in range(FRAMES)]
                if entering:
                    pair = [
                        (
                            v.astype(jnp.float32)
                            + 0.5 * nz[sec + 1, f, row - HALO + NEDGE].astype(jnp.float32)
                        ).astype(jnp.bfloat16)
                        for f, v in enumerate(pair)
                    ]
                for f in range(FRAMES):
                    lat_out[row, f] = pair[f]
                put_mixed(dst, row, k + 1, [v.astype(jnp.float32) for v in pair], slot + 2 * j)

        def several(bases):
            accs = [conv_of(base) for base in bases]
            for i, base in enumerate(bases):
                finish(base, accs[i], 4 * i)

        if bases is None:
            several([k % 3 + 2 * i for i in range(4 - k % 3)])
        else:
            several(bases)

    def edge_copy(sec, i):
        count = NSEC - sec
        lo, to, d = (
            (NEDGE, NEDGE + STRIP, -1),
            (NEDGE + STRIP - count, NEDGE - count, 1),
        )[i]
        return remote(nz.at[sec, :, pl.ds(lo, count)], nz.at[sec, :, pl.ds(to, count)],
                      n_send.at[sec, i], n_recv.at[sec, i], me, tile_at(d))

    def forward_noise(sec):
        arrived(later_noise(sec), x_recv.at[sec])
        for i in range(2):
            edge_copy(sec, i).start()

    def wait_edge(sec):
        for i in range(2):
            edge_copy(sec, i).wait_recv()

    near = (HALO + STRIP) * (1 - core)
    over = (HALO + STRIP) * core
    inner = (1 - core) * STRIP
    outer = core * STRIP

    mix_rows(0, HALO, STRIP)
    for row in range(HALO):
        arrived(entry.at[0, pl.ds(near + row, 1)], a_recv.at[row + core, core])
    mix_rows(0, near, HALO)
    own_weight.wait()
    finish_share(0)
    step(0, [inner, inner + 2])
    for row in range(HALO):
        arrived(entry.at[0, pl.ds(over + row, 1)], a_recv.at[row + 1 - core, 1 - core])
    mix_rows(0, over, HALO)
    blank_outside(0)
    step(0, [outer, outer + 2])
    blank_outside(1)
    forward_noise(2)
    forward_noise(3)
    step(1)
    blank_outside(0)
    arrived(later_noise(1), x_recv.at[1])
    step(2)
    for i in range(2):
        strip_copy(i).start()

    for sec in (1, 2, 3):
        start_share(sec)
    arrived(entry.at[1, pl.ds(near, HALO)], b_recv.at[core])
    mix_rows(3, near, HALO)
    finish_share(1)
    wait_edge(2)
    step(3, [inner, inner + 2])
    arrived(entry.at[1, pl.ds(over, HALO)], b_recv.at[1 - core])
    mix_rows(3, over, HALO)
    blank_outside(1)
    step(3, [outer, outer + 2])
    blank_outside(0)
    finish_share(2)
    wait_edge(3)
    step(4)
    blank_outside(1)
    finish_share(3)
    step(5)

    for d in (1, 2, 3):
        slice_to(d).wait_send()
    for i in range(2):
        strip_copy(i).wait_send()
        for sec in (2, 3):
            edge_copy(sec, i).wait_send()

    @pl.when(me == 0)
    def _():
        for row in ROW_ORDER:
            for d in (1, 2, 3):
                first_to(row, d).wait_send()

    @pl.when(me != 0)
    def _():
        for d in (1, 2, 3):
            later_to(d).wait_send()

    for sec in range(NSEC):
        @pl.when(me != sec)
        def _(sec=sec):
            for d in (1, 2, 3):
                gather(sec, d).wait_send()
            share(sec).wait_send()

    for row in range(STRIP):
        for i in goes(row):
            row_copy(row, i).wait_send()


def build(mesh, per_z):
    tiles = mesh.shape["tile"]
    bf = jnp.bfloat16
    dma = pltpu.SemaphoreType.DMA

    def per_device(latent_clips, augment_noise, section_weights, frame_mixing, step_embed):
        vmem = pl.BlockSpec(memory_space=pltpu.VMEM)
        hbm = pl.BlockSpec(memory_space=pltpu.HBM)
        return pl.pallas_call(
            functools.partial(kernel, tiles, per_z),
            out_shape=pltpu.VMEM(latent_clips.shape, bf),
            in_specs=[hbm, hbm, hbm, hbm, hbm],
            out_specs=vmem,
            scratch_shapes=[
                pltpu.VMEM((2, WIN, FRAMES, COLS, C), bf),
                pltpu.VMEM((WIN, FRAMES, COLS, C), bf),
                pltpu.VMEM((3, WIN, FRAMES, COLS, C), bf),
                pltpu.VMEM((3, WIN, FRAMES, COLS, C), bf),
                pltpu.VMEM((NSEC, FRAMES, NROWS, COLS, C), bf),
                pltpu.VMEM((NSEC, 9 * C, C), bf),
                pltpu.VMEM((FRAMES, STRIP, COLS, C), bf),
                pltpu.VMEM((NSTEP, C), jnp.float32),
                pltpu.VMEM((NSTEP, C), jnp.float32),
                pltpu.VMEM((SHIFTS, COLS + 16, C), jnp.float32),
                dma((STRIP, 4)), dma((STRIP,)),
                dma((4,)), dma((NSEC,)),
                dma((4,)), dma((NSEC,)),
                dma((NSEC, 4)), dma((NSEC, 4)),
                dma((NSEC,)), dma((NSEC,)),
                dma((STRIP, 2)), dma((STRIP, 2)),
                dma((2,)), dma((2,)),
                dma((NSEC, 2)), dma((NSEC, 2)),
                dma((4,)),
            ],
            compiler_params=pltpu.CompilerParams(
                collective_id=0, has_side_effects=True, vmem_limit_bytes=61 << 20
            ),
        )(latent_clips, augment_noise, section_weights, frame_mixing, step_embed)

    return jax.shard_map(
        per_device,
        mesh=mesh,
        in_specs=(
            P("segment", None, "tile", None, None),
            P("segment", None, None, "tile", None, None),
            P("segment", None, None),
            P(),
            P(),
        ),
        out_specs=P("segment", None, "tile", None, None),
        check_vma=False,
    )


def solution(mesh):
    return build(mesh, 8)
```

```python
import functools

import jax
import jax.numpy as jnp
from jax import lax
from jax.experimental import pallas as pl
from jax.experimental.pallas import tpu as pltpu
from jax.sharding import PartitionSpec as P

MESH = pl.DeviceIdType.MESH
C = 128
COLS = 128
FRAMES = 2
STRIP = 4
HALO = 3
WIN = STRIP + 2 * HALO
NSEC = 4
NSTEP = 6
SECTION = (0, 0, 0, 1, 2, 3)
NEDGE = 2
NROWS = STRIP + 2 * NEDGE
SLICE = 9 * C // 8
SHIFTS = 12
ROW_ORDER = (1, 2, 0, 3)

norm_eps = 1e-06


def kernel(tiles, per_z, latent_hbm, noise_ref, weight_ref, mix_hbm, emb_hbm, out_ref,
           entry, lat, mxa, mxb, nz, wts, latent_ref, mix_ref, emb_ref, shift,
           f_send, f_recv, x_send, x_recv, wx_send, wx_recv, wz_send, wz_recv, wc_send, wc_recv,
           a_send, a_recv, b_send, b_recv, n_send, n_recv, own_sem):
    me = lax.axis_index("segment")
    t = lax.axis_index("tile")
    core = lax.rem(t, 2)
    zq = lax.rem(t // per_z, 4)
    part = core * 4 + zq
    partner = t + 1 - 2 * core
    mx = (mxa, mxb)

    def tile_at(d):
        return lax.rem(t + d + tiles, tiles)

    def seg_at(d):
        return lax.rem(me + d, NSEC)

    def quad_at(d):
        return t + (lax.rem(zq + d, 4) - zq) * per_z

    def remote(src, dst, send, recv, seg, tile):
        return pltpu.make_async_remote_copy(
            src_ref=src,
            dst_ref=dst,
            send_sem=send,
            recv_sem=recv,
            device_id=(seg, tile),
            device_id_type=MESH,
        )

    def arrived(ref, sem):
        pltpu.make_async_copy(ref, ref, sem).wait()

    barrier = pltpu.get_barrier_semaphore()
    others = [(seg_at(d), t) for d in (1, 2, 3)]
    others += [(me, quad_at(d)) for d in (1, 2, 3)]
    others += [(me, tile_at(d)) for d in (-1, 1)]
    for dev in others:
        pl.semaphore_signal(barrier, inc=1, device_id=dev, device_id_type=MESH)

    def first_noise(row):
        return nz.at[0, :, pl.ds(NEDGE + row, 1)]

    def later_noise(sec):
        return nz.at[sec, :, pl.ds(NEDGE, STRIP)]

    own_weight = pltpu.make_async_copy(weight_ref.at[0], wts.at[me], own_sem.at[0])
    own_rest = [
        pltpu.make_async_copy(latent_hbm.at[0], latent_ref, own_sem.at[1]),
        pltpu.make_async_copy(mix_hbm, mix_ref, own_sem.at[2]),
        pltpu.make_async_copy(emb_hbm, emb_ref, own_sem.at[3]),
    ]
    for c in own_rest:
        c.start()

    @pl.when(me == 0)
    def _():
        for row in ROW_ORDER:
            pltpu.make_async_copy(
                noise_ref.at[0, me, :, pl.ds(row, 1)], first_noise(row), f_recv.at[row]
            ).start()

    @pl.when(me != 0)
    def _():
        pltpu.make_async_copy(noise_ref.at[0, me], later_noise(me), x_recv.at[me]).start()

    own_weight.start()
    for side in (0, COLS + 8):
        shift[:, pl.ds(side, 8)] = jnp.zeros((SHIFTS, 8, C), jnp.float32)
    pl.semaphore_wait(barrier, len(others))

    rows_of = pl.ds(pl.multiple_of(part * SLICE, 16), SLICE)
    half = pl.ds(pl.multiple_of(core * 4 * SLICE, 16), 4 * SLICE)

    def slice_to(d):
        return remote(weight_ref.at[0, rows_of], wts.at[me, rows_of],
                      wx_send.at[d], wx_recv.at[me], seg_at(d), t)

    def first_to(row, d):
        return remote(noise_ref.at[0, seg_at(d), :, pl.ds(row, 1)], first_noise(row),
                      f_send.at[row, d], f_recv.at[row], seg_at(d), t)

    def later_to(d):
        return remote(noise_ref.at[0, seg_at(d)], later_noise(me),
                      x_send.at[d], x_recv.at[me], seg_at(d), t)

    def gather(sec, d):
        return remote(wts.at[sec, rows_of], wts.at[sec, rows_of],
                      wz_send.at[sec, d], wz_recv.at[sec, d], me, quad_at(d))

    def share(sec):
        return remote(wts.at[sec, half], wts.at[sec, half],
                      wc_send.at[sec], wc_recv.at[sec], me, partner)

    for d in (2, 1, 3):
        slice_to(d).start()

    @pl.when(me == 0)
    def _():
        for row in ROW_ORDER:
            for d in (2, 1, 3):
                first_to(row, d).start()

    for sec, early in ((1, (3, 2, 1)), (2, (2, 1, 3)), (3, (1, 3, 2))):
        @pl.when(me == sec)
        def _(early=early):
            for d in early:
                later_to(d).start()

    def start_gather(sec):
        @pl.when(me != sec)
        def _():
            arrived(wts.at[sec, rows_of], wx_recv.at[sec])
            for d in (1, 2, 3):
                gather(sec, d).start()

    def start_share(sec):
        @pl.when(me != sec)
        def _():
            for d in (1, 2, 3):
                gather(sec, d).wait_recv()
            share(sec).start()

    def finish_share(sec):
        @pl.when(me != sec)
        def _():
            share(sec).wait_recv()

    for sec in range(NSEC):
        start_gather(sec)

    def row_copy(row, i):
        to, d = ((HALO + STRIP + row, -1), (row - 1, 1))[i]
        return remote(entry.at[0, pl.ds(HALO + row, 1)], entry.at[0, pl.ds(to, 1)],
                      a_send.at[row, i], a_recv.at[row, i], me, tile_at(d))

    def goes(row):
        return [i for i in range(2) if 0 <= row - i < HALO]

    def strip_copy(i):
        lo = (HALO + 2 * core, HALO + 2 - core, HALO + 1 - core)[i]
        count = (2, 1, HALO)[i]
        away = STRIP - 2 * STRIP * core
        to, device = (lo + away, tile_at(2 * core - 1)) if i < 2 else (lo - away, partner)
        return remote(entry.at[1, pl.ds(lo, count)], entry.at[1, pl.ds(to, count)],
                      b_send.at[i], b_recv.at[i], me, device)

    for c in own_rest:
        c.wait()
    for row in ROW_ORDER:
        arrived(first_noise(row), f_recv.at[row])
        for f in range(FRAMES):
            entry[0, HALO + row, f] = (
                latent_ref[f, row].astype(jnp.float32)
                + 0.5 * nz[0, f, NEDGE + row].astype(jnp.float32)
            ).astype(jnp.bfloat16)
        for i in goes(row):
            row_copy(row, i).start()

    start_share(0)

    def put_mixed(dst, row, k, pair, slot):
        change = (0.5 * mix_ref[k:k + 1, :]) * (pair[1] - pair[0])
        for f, mixed in enumerate((pair[0] + change, pair[1] - change)):
            wide = shift.at[slot + f]
            wide[pl.ds(8, COLS)] = mixed
            mx[dst][1, row, f] = mixed.astype(jnp.bfloat16)
            mx[dst][0, row, f] = wide[pl.ds(7, COLS)].astype(jnp.bfloat16)
            mx[dst][2, row, f] = wide[pl.ds(9, COLS)].astype(jnp.bfloat16)

    def blank_outside(dst):
        zero = jnp.zeros((3, HALO, FRAMES, COLS, C), jnp.bfloat16)

        @pl.when(t == 0)
        def _():
            mx[dst][:, pl.ds(0, HALO)] = zero

        @pl.when(t == tiles - 1)
        def _():
            mx[dst][:, pl.ds(HALO + STRIP, HALO)] = zero

    def mix_rows(k, lo, count):
        for j in range(count):
            put_mixed(
                k % 2, lo + j, k,
                [entry[k // 3, lo + j, f].astype(jnp.float32) for f in range(FRAMES)], 2 * j,
            )

    def step(k, bases=None):
        sec = SECTION[k]
        src, dst = k % 2, (k + 1) % 2
        lat_in = entry.at[k // 3] if k % 3 == 0 else lat
        lat_out = entry.at[1] if k == 2 else lat
        entering = k + 1 < NSTEP and SECTION[k + 1] != sec

        def conv_of(base):
            lhs = jnp.concatenate(
                [
                    mx[src][b, base + i].reshape(FRAMES * COLS, C)
                    for i in range(4)
                    for b in range(3)
                ],
                axis=1,
            )
            w = wts[sec]
            none = jnp.zeros((3 * C, C), jnp.bfloat16)
            rhs = jnp.concatenate(
                [jnp.concatenate([w, none], axis=0), jnp.concatenate([none, w], axis=0)], axis=1
            )
            return jnp.dot(lhs, rhs, preferred_element_type=jnp.float32)

        def finish(base, acc, slot):
            for j in range(2):
                row = base + 1 + j
                conv = acc[:, j * C:(j + 1) * C] + emb_ref[k:k + 1, :]
                power = jnp.sum(conv * conv, axis=-1, keepdims=True)
                half = conv * lax.rsqrt(power * (4.0 / C) + 4.0 * norm_eps)
                old = lat_in[row].reshape(FRAMES * COLS, C).astype(jnp.float32)
                new = (0.9 * old + (0.5 * half) * (1.0 + jnp.tanh(half))).astype(jnp.bfloat16)
                if k == NSTEP - 1:
                    for f in range(FRAMES):
                        out_ref[0, f, row - HALO] = new[f * COLS:(f + 1) * COLS]
                    continue
                pair = [new[f * COLS:(f + 1) * COLS] for f in range(FRAMES)]
                if entering:
                    pair = [
                        (
                            v.astype(jnp.float32)
                            + 0.5 * nz[sec + 1, f, row - HALO + NEDGE].astype(jnp.float32)
                        ).astype(jnp.bfloat16)
                        for f, v in enumerate(pair)
                    ]
                for f in range(FRAMES):
                    lat_out[row, f] = pair[f]
                put_mixed(dst, row, k + 1, [v.astype(jnp.float32) for v in pair], slot + 2 * j)

        def several(bases):
            accs = [conv_of(base) for base in bases]
            for i, base in enumerate(bases):
                finish(base, accs[i], 4 * i)

        if bases is None:
            several([k % 3 + 2 * i for i in range(4 - k % 3)])
        else:
            several(bases)

    def edge_copy(sec, i):
        count = NSEC - sec
        lo, to, d = (
            (NEDGE, NEDGE + STRIP, -1),
            (NEDGE + STRIP - count, NEDGE - count, 1),
        )[i]
        return remote(nz.at[sec, :, pl.ds(lo, count)], nz.at[sec, :, pl.ds(to, count)],
                      n_send.at[sec, i], n_recv.at[sec, i], me, tile_at(d))

    def forward_noise(sec):
        arrived(later_noise(sec), x_recv.at[sec])
        for i in range(2):
            edge_copy(sec, i).start()

    def wait_edge(sec):
        for i in range(2):
            edge_copy(sec, i).wait_recv()

    near = (HALO + STRIP) * (1 - core)
    over = (HALO + STRIP) * core
    inner = (1 - core) * STRIP
    outer = core * STRIP

    mix_rows(0, HALO, STRIP)
    for row in range(HALO):
        arrived(entry.at[0, pl.ds(near + row, 1)], a_recv.at[row + core, core])
    mix_rows(0, near, HALO)
    own_weight.wait()
    finish_share(0)
    step(0, [inner, inner + 2])
    for row in range(HALO):
        arrived(entry.at[0, pl.ds(over + row, 1)], a_recv.at[row + 1 - core, 1 - core])
    mix_rows(0, over, HALO)
    blank_outside(0)
    step(0, [outer, outer + 2])
    blank_outside(1)
    forward_noise(2)
    forward_noise(3)
    step(1)
    blank_outside(0)
    arrived(later_noise(1), x_recv.at[1])
    step(2, [2 + 2 * core])
    strip_copy(0).start()
    step(2, [4 - 2 * core])
    strip_copy(1).start()
    strip_copy(2).start()

    for sec in (1, 2, 3):
        start_share(sec)
    arrived(entry.at[1, pl.ds(near, HALO)], b_recv.at[2])
    mix_rows(3, near, HALO)
    finish_share(1)
    wait_edge(2)
    step(3, [inner, inner + 2])
    arrived(entry.at[1, pl.ds(over + 1 - core, 2)], b_recv.at[0])
    mix_rows(3, over + 1 - core, 2)
    blank_outside(1)
    step(3, [outer + 2 - 2 * core])
    arrived(entry.at[1, pl.ds(over + 2 * core, 1)], b_recv.at[1])
    mix_rows(3, over + 2 * core, 1)
    blank_outside(1)
    step(3, [outer + 2 * core])
    blank_outside(0)
    finish_share(2)
    wait_edge(3)
    step(4)
    blank_outside(1)
    finish_share(3)
    step(5)

    for d in (1, 2, 3):
        slice_to(d).wait_send()
    for i in range(3):
        strip_copy(i).wait_send()
    for i in range(2):
        for sec in (2, 3):
            edge_copy(sec, i).wait_send()

    @pl.when(me == 0)
    def _():
        for row in ROW_ORDER:
            for d in (1, 2, 3):
                first_to(row, d).wait_send()

    @pl.when(me != 0)
    def _():
        for d in (1, 2, 3):
            later_to(d).wait_send()

    for sec in range(NSEC):
        @pl.when(me != sec)
        def _(sec=sec):
            for d in (1, 2, 3):
                gather(sec, d).wait_send()
            share(sec).wait_send()

    for row in range(STRIP):
        for i in goes(row):
            row_copy(row, i).wait_send()


def build(mesh, per_z):
    tiles = mesh.shape["tile"]
    bf = jnp.bfloat16
    dma = pltpu.SemaphoreType.DMA

    def per_device(latent_clips, augment_noise, section_weights, frame_mixing, step_embed):
        vmem = pl.BlockSpec(memory_space=pltpu.VMEM)
        hbm = pl.BlockSpec(memory_space=pltpu.HBM)
        return pl.pallas_call(
            functools.partial(kernel, tiles, per_z),
            out_shape=pltpu.VMEM(latent_clips.shape, bf),
            in_specs=[hbm, hbm, hbm, hbm, hbm],
            out_specs=vmem,
            scratch_shapes=[
                pltpu.VMEM((2, WIN, FRAMES, COLS, C), bf),
                pltpu.VMEM((WIN, FRAMES, COLS, C), bf),
                pltpu.VMEM((3, WIN, FRAMES, COLS, C), bf),
                pltpu.VMEM((3, WIN, FRAMES, COLS, C), bf),
                pltpu.VMEM((NSEC, FRAMES, NROWS, COLS, C), bf),
                pltpu.VMEM((NSEC, 9 * C, C), bf),
                pltpu.VMEM((FRAMES, STRIP, COLS, C), bf),
                pltpu.VMEM((NSTEP, C), jnp.float32),
                pltpu.VMEM((NSTEP, C), jnp.float32),
                pltpu.VMEM((SHIFTS, COLS + 16, C), jnp.float32),
                dma((STRIP, 4)), dma((STRIP,)),
                dma((4,)), dma((NSEC,)),
                dma((4,)), dma((NSEC,)),
                dma((NSEC, 4)), dma((NSEC, 4)),
                dma((NSEC,)), dma((NSEC,)),
                dma((STRIP, 2)), dma((STRIP, 2)),
                dma((3,)), dma((3,)),
                dma((NSEC, 2)), dma((NSEC, 2)),
                dma((4,)),
            ],
            compiler_params=pltpu.CompilerParams(
                collective_id=0, has_side_effects=True, vmem_limit_bytes=61 << 20
            ),
        )(latent_clips, augment_noise, section_weights, frame_mixing, step_embed)

    return jax.shard_map(
        per_device,
        mesh=mesh,
        in_specs=(
            P("segment", None, "tile", None, None),
            P("segment", None, None, "tile", None, None),
            P("segment", None, None),
            P(),
            P(),
        ),
        out_specs=P("segment", None, "tile", None, None),
        check_vma=False,
    )


def solution(mesh):
    return build(mesh, 8)
```

```python
import functools

import jax
import jax.numpy as jnp
from jax import lax
from jax.experimental import pallas as pl
from jax.experimental.pallas import tpu as pltpu
from jax.sharding import PartitionSpec as P

MESH = pl.DeviceIdType.MESH
C = 128
COLS = 128
FRAMES = 2
STRIP = 4
HALO = 3
WIN = STRIP + 2 * HALO
NSEC = 4
NSTEP = 6
SECTION = (0, 0, 0, 1, 2, 3)
NEDGE = 2
NROWS = STRIP + 2 * NEDGE
SLICE = 9 * C // 8
SHIFTS = 12
ROW_ORDER = (1, 2, 0, 3)

norm_eps = 1e-06


def kernel(tiles, per_z, latent_hbm, noise_ref, weight_ref, mix_hbm, emb_hbm, out_ref,
           entry, lat, mxa, mxb, nz, wts, latent_ref, mix_ref, emb_ref, shift,
           f_send, f_recv, x_send, x_recv, wx_send, wx_recv, wz_send, wz_recv, wc_send, wc_recv,
           a_send, a_recv, b_send, b_recv, n_send, n_recv, own_sem):
    me = lax.axis_index("segment")
    t = lax.axis_index("tile")
    core = lax.rem(t, 2)
    zq = lax.rem(t // per_z, 4)
    part = core * 4 + zq
    partner = t + 1 - 2 * core
    mx = (mxa, mxb)

    def tile_at(d):
        return lax.rem(t + d + tiles, tiles)

    def seg_at(d):
        return lax.rem(me + d, NSEC)

    def quad_at(d):
        return t + (lax.rem(zq + d, 4) - zq) * per_z

    def remote(src, dst, send, recv, seg, tile):
        return pltpu.make_async_remote_copy(
            src_ref=src,
            dst_ref=dst,
            send_sem=send,
            recv_sem=recv,
            device_id=(seg, tile),
            device_id_type=MESH,
        )

    def arrived(ref, sem):
        pltpu.make_async_copy(ref, ref, sem).wait()

    barrier = pltpu.get_barrier_semaphore()
    others = [(seg_at(d), t) for d in (1, 2, 3)]
    others += [(me, quad_at(d)) for d in (1, 2, 3)]
    others += [(me, tile_at(d)) for d in (-1, 1)]
    for dev in others:
        pl.semaphore_signal(barrier, inc=1, device_id=dev, device_id_type=MESH)

    def first_noise(row):
        return nz.at[0, :, pl.ds(NEDGE + row, 1)]

    def later_noise(sec):
        return nz.at[sec, :, pl.ds(NEDGE, STRIP)]

    own_weight = pltpu.make_async_copy(weight_ref.at[0], wts.at[me], own_sem.at[0])
    own_rest = [
        pltpu.make_async_copy(latent_hbm.at[0], latent_ref, own_sem.at[1]),
        pltpu.make_async_copy(mix_hbm, mix_ref, own_sem.at[2]),
        pltpu.make_async_copy(emb_hbm, emb_ref, own_sem.at[3]),
    ]
    for c in own_rest:
        c.start()

    @pl.when(me == 0)
    def _():
        for row in ROW_ORDER:
            pltpu.make_async_copy(
                noise_ref.at[0, me, :, pl.ds(row, 1)], first_noise(row), f_recv.at[row]
            ).start()

    @pl.when(me != 0)
    def _():
        pltpu.make_async_copy(noise_ref.at[0, me], later_noise(me), x_recv.at[me]).start()

    own_weight.start()
    for side in (0, COLS + 8):
        shift[:, pl.ds(side, 8)] = jnp.zeros((SHIFTS, 8, C), jnp.float32)
    pl.semaphore_wait(barrier, len(others))

    rows_of = pl.ds(pl.multiple_of(part * SLICE, 16), SLICE)
    half = pl.ds(pl.multiple_of(core * 4 * SLICE, 16), 4 * SLICE)

    def slice_to(d):
        return remote(weight_ref.at[0, rows_of], wts.at[me, rows_of],
                      wx_send.at[d], wx_recv.at[me], seg_at(d), t)

    def first_to(row, d):
        return remote(noise_ref.at[0, seg_at(d), :, pl.ds(row, 1)], first_noise(row),
                      f_send.at[row, d], f_recv.at[row], seg_at(d), t)

    def later_to(d):
        return remote(noise_ref.at[0, seg_at(d)], later_noise(me),
                      x_send.at[d], x_recv.at[me], seg_at(d), t)

    def gather(sec, d):
        return remote(wts.at[sec, rows_of], wts.at[sec, rows_of],
                      wz_send.at[sec, d], wz_recv.at[sec, d], me, quad_at(d))

    def share(sec):
        return remote(wts.at[sec, half], wts.at[sec, half],
                      wc_send.at[sec], wc_recv.at[sec], me, partner)

    for d in (2, 1, 3):
        slice_to(d).start()

    @pl.when(me == 0)
    def _():
        for row in ROW_ORDER:
            for d in (2, 1, 3):
                first_to(row, d).start()

    for sec, early in ((1, (3, 1)), (2, (2, 1, 3)), (3, (1, 3))):
        @pl.when(me == sec)
        def _(early=early):
            for d in early:
                later_to(d).start()

    def start_gather(sec):
        @pl.when(me != sec)
        def _():
            arrived(wts.at[sec, rows_of], wx_recv.at[sec])
            for d in (1, 2, 3):
                gather(sec, d).start()

    def start_share(sec):
        @pl.when(me != sec)
        def _():
            for d in (1, 2, 3):
                gather(sec, d).wait_recv()
            share(sec).start()

    def finish_share(sec):
        @pl.when(me != sec)
        def _():
            share(sec).wait_recv()

    for sec in range(NSEC):
        start_gather(sec)

    def row_copy(row, i):
        to, d = ((HALO + STRIP + row, -1), (row - 1, 1))[i]
        return remote(entry.at[0, pl.ds(HALO + row, 1)], entry.at[0, pl.ds(to, 1)],
                      a_send.at[row, i], a_recv.at[row, i], me, tile_at(d))

    def goes(row):
        return [i for i in range(2) if 0 <= row - i < HALO]

    def strip_copy(i):
        lo = (HALO + 2 * core, HALO + 2 - core, HALO + 1 - core)[i]
        count = (2, 1, HALO)[i]
        away = STRIP - 2 * STRIP * core
        to, device = (lo + away, tile_at(2 * core - 1)) if i < 2 else (lo - away, partner)
        return remote(entry.at[1, pl.ds(lo, count)], entry.at[1, pl.ds(to, count)],
                      b_send.at[i], b_recv.at[i], me, device)

    for c in own_rest:
        c.wait()
    for row in ROW_ORDER:
        arrived(first_noise(row), f_recv.at[row])
        for f in range(FRAMES):
            entry[0, HALO + row, f] = (
                latent_ref[f, row].astype(jnp.float32)
                + 0.5 * nz[0, f, NEDGE + row].astype(jnp.float32)
            ).astype(jnp.bfloat16)
        for i in goes(row):
            row_copy(row, i).start()

    @pl.when(lax.rem(me, 2) == 1)
    def _():
        later_to(2).start()

    start_share(0)

    def put_mixed(dst, row, k, pair, slot):
        change = (0.5 * mix_ref[k:k + 1, :]) * (pair[1] - pair[0])
        for f, mixed in enumerate((pair[0] + change, pair[1] - change)):
            wide = shift.at[slot + f]
            wide[pl.ds(8, COLS)] = mixed
            mx[dst][1, row, f] = mixed.astype(jnp.bfloat16)
            mx[dst][0, row, f] = wide[pl.ds(7, COLS)].astype(jnp.bfloat16)
            mx[dst][2, row, f] = wide[pl.ds(9, COLS)].astype(jnp.bfloat16)

    def blank_outside(dst):
        zero = jnp.zeros((3, HALO, FRAMES, COLS, C), jnp.bfloat16)

        @pl.when(t == 0)
        def _():
            mx[dst][:, pl.ds(0, HALO)] = zero

        @pl.when(t == tiles - 1)
        def _():
            mx[dst][:, pl.ds(HALO + STRIP, HALO)] = zero

    def mix_rows(k, lo, count):
        for j in range(count):
            put_mixed(
                k % 2, lo + j, k,
                [entry[k // 3, lo + j, f].astype(jnp.float32) for f in range(FRAMES)], 2 * j,
            )

    def step(k, bases=None):
        sec = SECTION[k]
        src, dst = k % 2, (k + 1) % 2
        lat_in = entry.at[k // 3] if k % 3 == 0 else lat
        lat_out = entry.at[1] if k == 2 else lat
        entering = k + 1 < NSTEP and SECTION[k + 1] != sec

        def conv_of(base):
            lhs = jnp.concatenate(
                [
                    mx[src][b, base + i].reshape(FRAMES * COLS, C)
                    for i in range(4)
                    for b in range(3)
                ],
                axis=1,
            )
            w = wts[sec]
            none = jnp.zeros((3 * C, C), jnp.bfloat16)
            rhs = jnp.concatenate(
                [jnp.concatenate([w, none], axis=0), jnp.concatenate([none, w], axis=0)], axis=1
            )
            return jnp.dot(lhs, rhs, preferred_element_type=jnp.float32)

        def finish(base, acc, slot):
            for j in range(2):
                row = base + 1 + j
                conv = acc[:, j * C:(j + 1) * C] + emb_ref[k:k + 1, :]
                power = jnp.sum(conv * conv, axis=-1, keepdims=True)
                half = conv * lax.rsqrt(power * (4.0 / C) + 4.0 * norm_eps)
                old = lat_in[row].reshape(FRAMES * COLS, C).astype(jnp.float32)
                new = (0.9 * old + (0.5 * half) * (1.0 + jnp.tanh(half))).astype(jnp.bfloat16)
                if k == NSTEP - 1:
                    for f in range(FRAMES):
                        out_ref[0, f, row - HALO] = new[f * COLS:(f + 1) * COLS]
                    continue
                pair = [new[f * COLS:(f + 1) * COLS] for f in range(FRAMES)]
                if entering:
                    pair = [
                        (
                            v.astype(jnp.float32)
                            + 0.5 * nz[sec + 1, f, row - HALO + NEDGE].astype(jnp.float32)
                        ).astype(jnp.bfloat16)
                        for f, v in enumerate(pair)
                    ]
                for f in range(FRAMES):
                    lat_out[row, f] = pair[f]
                put_mixed(dst, row, k + 1, [v.astype(jnp.float32) for v in pair], slot + 2 * j)

        def several(bases):
            accs = [conv_of(base) for base in bases]
            for i, base in enumerate(bases):
                finish(base, accs[i], 4 * i)

        if bases is None:
            several([k % 3 + 2 * i for i in range(4 - k % 3)])
        else:
            several(bases)

    def edge_copy(sec, i):
        count = NSEC - sec
        lo, to, d = (
            (NEDGE, NEDGE + STRIP, -1),
            (NEDGE + STRIP - count, NEDGE - count, 1),
        )[i]
        return remote(nz.at[sec, :, pl.ds(lo, count)], nz.at[sec, :, pl.ds(to, count)],
                      n_send.at[sec, i], n_recv.at[sec, i], me, tile_at(d))

    def forward_noise(sec):
        arrived(later_noise(sec), x_recv.at[sec])
        for i in range(2):
            edge_copy(sec, i).start()

    def wait_edge(sec):
        for i in range(2):
            edge_copy(sec, i).wait_recv()

    near = (HALO + STRIP) * (1 - core)
    over = (HALO + STRIP) * core
    inner = (1 - core) * STRIP
    outer = core * STRIP

    mix_rows(0, HALO, STRIP)
    for row in range(HALO):
        arrived(entry.at[0, pl.ds(near + row, 1)], a_recv.at[row + core, core])
    mix_rows(0, near, HALO)
    own_weight.wait()
    finish_share(0)
    step(0, [inner, inner + 2])
    for row in range(HALO):
        arrived(entry.at[0, pl.ds(over + row, 1)], a_recv.at[row + 1 - core, 1 - core])
    mix_rows(0, over, HALO)
    blank_outside(0)
    step(0, [outer, outer + 2])
    blank_outside(1)
    forward_noise(2)
    step(1)
    blank_outside(0)
    arrived(later_noise(1), x_recv.at[1])
    step(2, [2 + 2 * core])
    strip_copy(0).start()
    step(2, [4 - 2 * core])
    strip_copy(1).start()
    strip_copy(2).start()
    forward_noise(3)

    for sec in (1, 2, 3):
        start_share(sec)
    arrived(entry.at[1, pl.ds(near, HALO)], b_recv.at[2])
    mix_rows(3, near, HALO)
    finish_share(1)
    wait_edge(2)
    step(3, [inner, inner + 2])
    arrived(entry.at[1, pl.ds(over + 1 - core, 2)], b_recv.at[0])
    mix_rows(3, over + 1 - core, 2)
    blank_outside(1)
    step(3, [outer + 2 - 2 * core])
    arrived(entry.at[1, pl.ds(over + 2 * core, 1)], b_recv.at[1])
    mix_rows(3, over + 2 * core, 1)
    blank_outside(1)
    step(3, [outer + 2 * core])
    blank_outside(0)
    finish_share(2)
    wait_edge(3)
    step(4)
    blank_outside(1)
    finish_share(3)
    step(5)

    for d in (1, 2, 3):
        slice_to(d).wait_send()
    for i in range(3):
        strip_copy(i).wait_send()
    for i in range(2):
        for sec in (2, 3):
            edge_copy(sec, i).wait_send()

    @pl.when(me == 0)
    def _():
        for row in ROW_ORDER:
            for d in (1, 2, 3):
                first_to(row, d).wait_send()

    @pl.when(me != 0)
    def _():
        for d in (1, 2, 3):
            later_to(d).wait_send()

    for sec in range(NSEC):
        @pl.when(me != sec)
        def _(sec=sec):
            for d in (1, 2, 3):
                gather(sec, d).wait_send()
            share(sec).wait_send()

    for row in range(STRIP):
        for i in goes(row):
            row_copy(row, i).wait_send()


def build(mesh, per_z):
    tiles = mesh.shape["tile"]
    bf = jnp.bfloat16
    dma = pltpu.SemaphoreType.DMA

    def per_device(latent_clips, augment_noise, section_weights, frame_mixing, step_embed):
        vmem = pl.BlockSpec(memory_space=pltpu.VMEM)
        hbm = pl.BlockSpec(memory_space=pltpu.HBM)
        return pl.pallas_call(
            functools.partial(kernel, tiles, per_z),
            out_shape=pltpu.VMEM(latent_clips.shape, bf),
            in_specs=[hbm, hbm, hbm, hbm, hbm],
            out_specs=vmem,
            scratch_shapes=[
                pltpu.VMEM((2, WIN, FRAMES, COLS, C), bf),
                pltpu.VMEM((WIN, FRAMES, COLS, C), bf),
                pltpu.VMEM((3, WIN, FRAMES, COLS, C), bf),
                pltpu.VMEM((3, WIN, FRAMES, COLS, C), bf),
                pltpu.VMEM((NSEC, FRAMES, NROWS, COLS, C), bf),
                pltpu.VMEM((NSEC, 9 * C, C), bf),
                pltpu.VMEM((FRAMES, STRIP, COLS, C), bf),
                pltpu.VMEM((NSTEP, C), jnp.float32),
                pltpu.VMEM((NSTEP, C), jnp.float32),
                pltpu.VMEM((SHIFTS, COLS + 16, C), jnp.float32),
                dma((STRIP, 4)), dma((STRIP,)),
                dma((4,)), dma((NSEC,)),
                dma((4,)), dma((NSEC,)),
                dma((NSEC, 4)), dma((NSEC, 4)),
                dma((NSEC,)), dma((NSEC,)),
                dma((STRIP, 2)), dma((STRIP, 2)),
                dma((3,)), dma((3,)),
                dma((NSEC, 2)), dma((NSEC, 2)),
                dma((4,)),
            ],
            compiler_params=pltpu.CompilerParams(
                collective_id=0, has_side_effects=True, vmem_limit_bytes=61 << 20
            ),
        )(latent_clips, augment_noise, section_weights, frame_mixing, step_embed)

    return jax.shard_map(
        per_device,
        mesh=mesh,
        in_specs=(
            P("segment", None, "tile", None, None),
            P("segment", None, None, "tile", None, None),
            P("segment", None, None),
            P(),
            P(),
        ),
        out_specs=P("segment", None, "tile", None, None),
        check_vma=False,
    )


def solution(mesh):
    return build(mesh, 8)
```
